32 devices in a mesh: groups: 2 (over x), row: 16 (over z, y, core).
Axes of the slice: x: 2, y: 2, z: 4, core: 2. Of those that a mesh axis runs over, the one named last changes fastest.
Arguments:
- basis: float32 [8192, 128], P(('groups', 'row')), parts along dimension 0, may hold values from -6 to 6
- springs: float32 [8192], P(('groups', 'row')), parts along dimension 0, may hold values from 0.25 to 8
- tangent_blocks: float32 [4096, 4096], P(('groups', 'row')), parts along dimension 0, may hold values from -0.375 to 0.375
- tile_rows: int32 [4096], P(('groups', 'row')), parts along dimension 0, may hold values from 0 to 3
- tile_owner: int32 [4096, 1], P(('groups', 'row')), parts along dimension 0, may hold values from 0 to 15, as said below
- tile_offset: int32 [4096], P(('groups', 'row')), parts along dimension 0, may hold values from 0 to 3
- tile_count: int32 [32], P(('groups', 'row')), parts along dimension 0, may hold values from 32 to 128, as said below
Outputs:
- stiff_image: float32 [8192, 128], P(('groups', 'row')), parts along dimension 0
- reduced: float32 [256, 128], P('groups'), parts along dimension 0
The draws below stay inside these ranges and needn't reach their ends.
There are 2 independent parts, one for each index of `groups`. The reference program is written for one: setup_inputs(seed, part) draws one part's arguments, and reference() takes and returns one part's arrays. A program takes and returns all parts, laid end to end along the dimension named above; each array names one. Nothing has to cross between parts.
Inputs may be any that keep to these rules, and one draw needn't show every extreme that they name: The first tile_count[d] slots of device d are live; some device has exactly 128. `tile_owner`: the slab is closed into a shell: every slot of device d names owner (d + o) mod 16 with o one of 0, 1, -1, 4, -4, 5, -5, 8. Among the slots of one device no owner appears more than 32 times, and owner d itself appears exactly 32 times in every device.
All inputs are finite; a program needn't handle non-finite values.
Results may differ from the reference program's by a relative error of at most 0.0003.
Values sent between devices are 32-bit elements; how exact they have to be, the bound alone decides.
A program may use at most 128 MiB of HBM per device.

```python
import math
import jax
import jax.numpy as jnp
from jax import lax

B = 64
MODES = 128
BR_DEV = 4
CAP = 128
MOST = 32
NB = 64
NDOF = 4096
SLOTS = 2048
N_ROW = 16


def draw_tile_count(key, part):
    first_key, second_key = jax.random.split(jax.random.fold_in(key, 17))
    counts = jax.random.randint(first_key, (N_ROW,), CAP // 4, CAP + 1)
    fullest = jax.random.randint(second_key, (), 0, N_ROW)
    return jnp.where(jnp.arange(N_ROW) == fullest, CAP, counts).astype(jnp.int32)


def draw_tile_owner(key, part):
    base_key = jax.random.fold_in(key, 29)
    steps_list = jnp.array([0, 1, -1, 4, -4, 5, -5, N_ROW // 2], dtype=jnp.int32)
    slot_ids = jnp.arange(CAP, dtype=jnp.int32)
    pattern = jnp.where(slot_ids < MOST, 0, 1 + (slot_ids - MOST) % 7).astype(jnp.int32)

    def one_device(device):
        order = jax.random.permutation(jax.random.fold_in(base_key, device), CAP)
        links = pattern[order]
        return ((device + steps_list[links]) % N_ROW).astype(jnp.int32)
    owners = jax.vmap(one_device)(jnp.arange(N_ROW, dtype=jnp.int32))
    return owners.reshape(SLOTS, 1).astype(jnp.int32)


def set_ends(entries, rng, smallest, top_value):
    extent = entries.shape
    place = [jax.random.randint(jax.random.fold_in(rng, axis), (), 0, extent[axis]) for axis in range(len(extent))]
    entries = entries.at[tuple(place)].set(smallest)
    longest = extent.index(max(extent))
    place[longest] = (place[longest] + 1) % extent[longest]
    return entries.at[tuple(place)].set(top_value)


def steps_of(key, extent, cuts, smallest, high):
    def one(axis_at, parts):
        heights = jax.random.uniform(jax.random.fold_in(jax.random.fold_in(key, 6), axis_at), (parts,), jnp.float32, smallest / len(cuts), high / len(cuts))
        return jnp.repeat(jnp.exp(heights), extent[axis_at] // parts).reshape((-1,) + (1,) * (len(extent) - axis_at - 1))

    factor_of = one(*cuts[0])
    for cut in cuts[1:]:
        factor_of = factor_of * one(*cut)
    return factor_of


def scatter_about(rng, shape, scale, reach, shards=(), kind=jnp.bfloat16):
    factor_of = steps_of(rng, shape, shards, -0.22, 0.18) if shards else 1.0
    drawn = jax.random.normal(rng, shape, jnp.float32) * scale * factor_of
    return jnp.minimum(jnp.maximum(drawn, -reach), reach).astype(kind)


def setup_inputs(seed: int = 0, part: int = 0) -> dict:
    streams_of = jax.random.split(jax.random.key(seed), 8)
    own_keys = jax.random.split(jax.random.fold_in(streams_of[7], part), 8)
    return {
        "basis": scatter_about(own_keys[0], (NDOF, MODES), 1.0, 6.0, ((0, 16),), jnp.float32),
        "springs": jnp.clip(jnp.exp(math.log(8.0) - 3.465736 * jax.random.uniform(own_keys[1], (NDOF,), jnp.float32) ** steps_of(own_keys[1], (NDOF,), ((0, 16),), -0.2, 0.2)), 0.25, 8.0),
        "tangent_blocks": scatter_about(own_keys[2], (SLOTS, B * B), 0.025, 0.375, ((0, 16),), jnp.float32),
        "tile_rows": set_ends(jax.random.randint(own_keys[3], (SLOTS,), 0, BR_DEV), jax.random.fold_in(own_keys[3], 1), 0, BR_DEV - 1).astype(jnp.int32),
        "tile_owner": draw_tile_owner(jax.random.fold_in(jax.random.fold_in(streams_of[7], part), 71), part),
        "tile_offset": set_ends(jax.random.randint(own_keys[5], (SLOTS,), 0, BR_DEV), jax.random.fold_in(own_keys[5], 1), 0, BR_DEV - 1).astype(jnp.int32),
        "tile_count": draw_tile_count(jax.random.fold_in(jax.random.fold_in(streams_of[7], part), 71), part),
    }


def reference(basis, springs, tangent_blocks, tile_rows, tile_owner, tile_offset, tile_count):
    basis_blocks = basis.reshape(NB, B, MODES)
    square_blocks = tangent_blocks.reshape(SLOTS, B, B)
    owner_ids = tile_owner[:, 0]
    devices = jnp.arange(N_ROW, dtype=jnp.int32)

    def one_device(device):
        first_slot = (device * CAP).astype(jnp.int32)
        blocks = lax.dynamic_slice_in_dim(square_blocks, first_slot, CAP, 0)
        rows_here = lax.dynamic_slice_in_dim(tile_rows, first_slot, CAP, 0)
        owners_here = lax.dynamic_slice_in_dim(owner_ids, first_slot, CAP, 0)
        offsets_here = lax.dynamic_slice_in_dim(tile_offset, first_slot, CAP, 0)
        columns = (owners_here * BR_DEV + offsets_here).astype(jnp.int32)
        picked = basis_blocks[columns]
        products = jnp.einsum('sij,sjk->sik', blocks, picked, precision=lax.Precision.HIGHEST)
        live_slot = (jnp.arange(CAP, dtype=jnp.int32) < tile_count[device]).astype(jnp.float32)
        row_select = (rows_here[None, :] == jnp.arange(BR_DEV, dtype=jnp.int32)[:, None]).astype(jnp.float32) * live_slot[None, :]
        return jnp.dot(row_select, products.reshape(CAP, B * MODES), precision=lax.Precision.HIGHEST)

    summed = lax.map(one_device, devices)
    stiff_image = springs[:, None] * basis + summed.reshape(NDOF, MODES)
    reduced = jnp.einsum('rm,rn->mn', basis, stiff_image, precision=lax.Precision.HIGHEST) / NDOF
    return stiff_image, reduced
```

```python
import functools

import jax
import jax.numpy as jnp
from jax import lax
from jax.experimental import pallas as pl
from jax.experimental.pallas import tpu as pltpu
from jax.sharding import PartitionSpec as P

B = 64
MODES = 128
BR_DEV = 4
CAP = 128
SUB = 16
F32, BF16 = jnp.float32, jnp.bfloat16


def split(x):
    hi = x.astype(BF16)
    return hi, (x - hi.astype(F32)).astype(BF16)


def mm(a, b):
    return jnp.dot(a, b, preferred_element_type=F32)


def mm3(a_hi, a_lo, b_hi, b_lo):
    both = mm(a_hi, jnp.concatenate([b_hi, b_lo], axis=1))
    return both[:, :MODES] + both[:, MODES:] + mm(a_lo, b_hi)


def kernel(
    n, dof_total,
    basis, springs, tangent, rows, owner, offset, count,
    stiff, reduced,
    shard, tang, dense_hi, dense_lo, acc, part, rs_buf, top_buf, red,
    loc_sem, send_sem, recv_sem, rs_send, rs_recv, top_send, top_recv, ag_send, ag_recv,
):
    me = lax.axis_index("row")
    steps = (0, 1, n - 1, 4, n - 4, 5, n - 5, n // 2)
    subs = n // SUB
    sub, pos = me // SUB, me % SUB

    def at(p):
        return {"row": p}

    def mate(s):
        return sub * SUB + (pos + s) % SUB

    barrier = pltpu.get_barrier_semaphore()
    greeted = [mate(s) for s in range(1, SUB)]
    if subs > 1:
        greeted += [(me + o) % n for o in steps[1:]] + [(me + SUB * q) % n for q in range(1, subs)]
    for p in greeted:
        pl.semaphore_signal(barrier, inc=1, device_id=at(p), device_id_type=pl.DeviceIdType.MESH)
    own_copy = pltpu.make_async_copy(basis, shard.at[0], loc_sem.at[0])
    own_copy.start()
    tang_copy = pltpu.make_async_copy(tangent, tang, loc_sem.at[1])
    tang_copy.start()
    pl.semaphore_wait(barrier, len(greeted))

    sends = []
    for k in (7, 5, 6, 3, 4, 1, 2):
        c = pltpu.make_async_remote_copy(
            basis, shard.at[k], send_sem.at[k], recv_sem.at[k],
            device_id=at((me + n - steps[k]) % n), device_id_type=pl.DeviceIdType.MESH,
        )
        c.start()
        sends.append((k, c))

    away = owner[...] - me
    away = jnp.where(away < 0, away + n, away)
    key = jnp.zeros_like(away)
    for k in range(1, 8):
        key = jnp.where(away == steps[k], k, key)
    place = key * 16 + offset[...] * 4 + rows[...]
    slot = lax.broadcasted_iota(jnp.int32, (1, CAP), 1)
    place = jnp.where(slot < count[0], place, -1)
    p_ids = lax.broadcasted_iota(jnp.int32, (CAP, CAP), 0)
    lane = lax.broadcasted_iota(jnp.int32, (CAP, CAP), 1)
    swapped = jnp.where((p_ids // 4) % 2 == 0, p_ids + 4, p_ids - 4)
    hot = jnp.concatenate([(p_ids == place), (swapped == place)], axis=0)
    hot = jnp.where(hot, 1.0, 0.0).astype(BF16)
    hot = jnp.concatenate([hot, hot], axis=1)
    keep = (p_ids // 4) % 2 == lane // B

    tang_copy.wait()

    def build(it, _):
        t = tang[:, pl.ds(pl.multiple_of(it * 256, 256), 256)]
        t_hi, t_lo = split(t)
        e = mm(hot, jnp.concatenate([t_hi, t_lo], axis=0))
        out = []
        for m in range(2):
            a = e[:CAP, m * 128:(m + 1) * 128]
            b = pltpu.roll(e[CAP:, m * 128:(m + 1) * 128], B, 1)
            out.append(jnp.where(keep, a, b))
        at_row = pl.ds(pl.multiple_of(it * 16, 16), 16)
        for cp in range(16):
            x = jnp.concatenate([out[0][cp * 8:cp * 8 + 8], out[1][cp * 8:cp * 8 + 8]], axis=0)
            hi, lo = split(x)
            dense_hi[at_row, cp * 128:(cp + 1) * 128] = hi
            dense_lo[at_row, cp * 128:(cp + 1) * 128] = lo
        return 0

    lax.fori_loop(0, 16, build, 0)

    own_copy.wait()
    own = shard[0]
    t_hi, t_lo = split(own.T)
    eye = p_ids == lane
    spring = jnp.concatenate(
        [jnp.sum(jnp.where(eye, springs[h:h + 1, :], 0.0), axis=1, keepdims=True) for h in range(2)], axis=0
    )
    scaled = spring * own

    def term(k, g):
        g_hi, g_lo = split(g)
        ks = slice(k * 256, (k + 1) * 256)
        return mm3(dense_hi[:, ks], dense_lo[:, ks], g_hi, g_lo)

    total = term(0, own)
    for k in (1, 2, 3, 4, 5, 6, 7):
        pltpu.make_async_copy(shard.at[k], shard.at[k], recv_sem.at[k]).wait()
        total = total + term(k, shard[k])
    acc[...] = total
    image = scaled + jnp.concatenate([acc[pl.ds(r, B, stride=BR_DEV), :] for r in range(BR_DEV)], axis=0)
    stiff[...] = image
    i_hi, i_lo = split(image)
    part[...] = (mm3(t_hi, t_lo, i_hi, i_lo) * (1.0 / dof_total)).reshape(SUB, 8, MODES)

    rs = []
    for s in range(1, SUB):
        c = pltpu.make_async_remote_copy(
            part.at[(pos + s) % SUB], rs_buf.at[s], rs_send.at[s], rs_recv.at[s],
            device_id=at(mate(s)), device_id_type=pl.DeviceIdType.MESH,
        )
        c.start()
        rs.append(c)
    mine = part[pos]
    for s in range(1, SUB):
        rs[s - 1].wait_recv()
        mine = mine + rs_buf[s]
    if subs > 1:
        top_buf[sub] = mine
        top = []
        for q in range(1, subs):
            c = pltpu.make_async_remote_copy(
                top_buf.at[sub], top_buf.at[sub], top_send.at[q], top_recv.at[q],
                device_id=at((me + SUB * q) % n), device_id_type=pl.DeviceIdType.MESH,
            )
            c.start()
            top.append(c)
        for c in top:
            c.wait_recv()
        mine = top_buf[0]
        for q in range(1, subs):
            mine = mine + top_buf[q]
    red[pos] = mine
    ag = []
    for s in range(1, SUB):
        c = pltpu.make_async_remote_copy(
            red.at[pos], red.at[pos], ag_send.at[s], ag_recv.at[s],
            device_id=at(mate(s)), device_id_type=pl.DeviceIdType.MESH,
        )
        c.start()
        ag.append(c)
    for c in ag:
        c.wait_recv()
    reduced[...] = red[...].reshape(MODES, MODES)
    for k, c in sends:
        c.wait_send()
    for c in rs + ag:
        c.wait_send()
    if subs > 1:
        for c in top:
            c.wait_send()


def shards(basis, springs, tangent_blocks, tile_rows, tile_owner, tile_offset, tile_count):
    n = lax.axis_size("row")
    dof_total = basis.shape[0] * n
    vm = pl.BlockSpec(memory_space=pltpu.VMEM)
    hbm = pl.BlockSpec(memory_space=pl.ANY)
    subs = max(n // SUB, 2)
    return pl.pallas_call(
        functools.partial(kernel, n, dof_total),
        out_shape=(
            jax.ShapeDtypeStruct((BR_DEV * B, MODES), F32),
            jax.ShapeDtypeStruct((MODES, MODES), F32),
        ),
        in_specs=[hbm, vm, hbm, vm, vm, vm, pl.BlockSpec(memory_space=pltpu.SMEM)],
        out_specs=(vm, vm),
        scratch_shapes=[
            pltpu.VMEM((8, BR_DEV * B, MODES), F32),
            pltpu.VMEM((CAP, B * B), F32),
            pltpu.VMEM((BR_DEV * B, 32 * B), BF16),
            pltpu.VMEM((BR_DEV * B, 32 * B), BF16),
            pltpu.VMEM((BR_DEV * B, MODES), F32),
            pltpu.VMEM((SUB, 8, MODES), F32),
            pltpu.VMEM((SUB, 8, MODES), F32),
            pltpu.VMEM((subs, 8, MODES), F32),
            pltpu.VMEM((SUB, 8, MODES), F32),
            pltpu.SemaphoreType.DMA((2,)),
            pltpu.SemaphoreType.DMA((8,)),
            pltpu.SemaphoreType.DMA((8,)),
            pltpu.SemaphoreType.DMA((SUB,)),
            pltpu.SemaphoreType.DMA((SUB,)),
            pltpu.SemaphoreType.DMA((subs,)),
            pltpu.SemaphoreType.DMA((subs,)),
            pltpu.SemaphoreType.DMA((SUB,)),
            pltpu.SemaphoreType.DMA((SUB,)),
        ],
        compiler_params=pltpu.CompilerParams(
            collective_id=0, has_side_effects=True, vmem_limit_bytes=32 * 1024 * 1024
        ),
    )(
        basis, springs.reshape(2, MODES), tangent_blocks,
        tile_rows.reshape(1, CAP), tile_owner.reshape(1, CAP), tile_offset.reshape(1, CAP), tile_count,
    )


def solution(mesh):
    in_specs = (
        P(("groups", "row"), None),
        P(("groups", "row")),
        P(("groups", "row"), None),
        P(("groups", "row")),
        P(("groups", "row"), None),
        P(("groups", "row")),
        P(("groups", "row")),
    )
    out_specs = (P(("groups", "row"), None), P("groups", None))
    return jax.shard_map(shards, mesh=mesh, in_specs=in_specs, out_specs=out_specs, check_vma=False)
```

```python
import functools

import jax
import jax.numpy as jnp
from jax import lax
from jax.experimental import pallas as pl
from jax.experimental.pallas import tpu as pltpu
from jax.sharding import PartitionSpec as P

B = 64
MODES = 128
BR_DEV = 4
CAP = 128
SUB = 16
F32, BF16 = jnp.float32, jnp.bfloat16


def split(x):
    hi = x.astype(BF16)
    return hi, (x - hi.astype(F32)).astype(BF16)


def mm(a, b):
    return jnp.dot(a, b, preferred_element_type=F32)


def mm3(a_hi, a_lo, b_hi, b_lo):
    both = mm(a_hi, jnp.concatenate([b_hi, b_lo], axis=1))
    return both[:, :MODES] + both[:, MODES:] + mm(a_lo, b_hi)


def kernel(
    n, dof_total,
    basis, springs_in, tangent, rows_in, owner_in, offset_in, count,
    stiff, reduced,
    springs, rows, owner, offset,
    shard, tang, dense_hi, dense_lo, acc, part, rs_buf, top_buf, red,
    loc_sem, send_sem, recv_sem, up_send, up_recv, down_send, down_recv, rs_send, rs_recv, top_send, top_recv, ag_send, ag_recv,
):
    me = lax.axis_index("row")
    steps = (0, 1, n - 1, 4, n - 4, 5, n - 5, n // 2)
    subs = n // SUB
    sub, pos = me // SUB, me % SUB

    def at(p):
        return {"row": p}

    def mate(s):
        return sub * SUB + (pos + s) % SUB

    barrier = pltpu.get_barrier_semaphore()
    greeted = [mate(s) for s in range(1, SUB)]
    if subs > 1:
        greeted += [(me + o) % n for o in steps[1:]] + [(me + SUB * q) % n for q in range(1, subs)]
    for p in greeted:
        pl.semaphore_signal(barrier, inc=1, device_id=at(p), device_id_type=pl.DeviceIdType.MESH)
    relayed = n == SUB
    z, q = me // 4, me % 4
    own_slot = z if relayed else 0
    own_copy = pltpu.make_async_copy(basis, shard.at[own_slot], loc_sem.at[0])
    own_copy.start()
    small = [
        pltpu.make_async_copy(x, y, loc_sem.at[2 + i])
        for i, (x, y) in enumerate(((springs_in, springs), (rows_in, rows), (owner_in, owner), (offset_in, offset)))
    ]
    for c in small:
        c.start()
    tang_copy = pltpu.make_async_copy(tangent, tang, loc_sem.at[1])
    tang_copy.start()
    pl.semaphore_wait(barrier, len(greeted))

    def remote(src, dst, s_sem, r_sem, p):
        return pltpu.make_async_remote_copy(
            src, dst, s_sem, r_sem, device_id=at(p), device_id_type=pl.DeviceIdType.MESH
        )

    def up(h):
        src = basis if h == 0 else shard.at[(z - h) % 4]
        return remote(src, shard.at[(z - h) % 4], up_send.at[h], up_recv.at[h], (me + 4) % n)

    def down(h):
        src = basis if h == 0 else shard.at[(z + h) % 4]
        return remote(src, shard.at[(z + h) % 4], down_send.at[h], down_recv.at[h], (me + n - 4) % n)

    first, last = jnp.where(q == 0, 1, 0), jnp.where(q == 3, 1, 0)
    gives = (
        (4, (z + first) % 4, z * 4 + (q + 3) % 4),
        (5, (z + 1 + first) % 4, z * 4 + (q + 3) % 4),
        (6, (z + 4 - last) % 4, z * 4 + (q + 1) % 4),
        (7, (z + 3 - last) % 4, z * 4 + (q + 1) % 4),
    )

    def give(h):
        for slot_id, whose, p in gives:
            far = jnp.where(whose < z, z - whose, whose - z)

            @pl.when(far == h)
            def _(slot_id=slot_id, whose=whose, p=p):
                src = basis if h == 0 else shard.at[whose]
                remote(src, shard.at[slot_id], send_sem.at[slot_id], recv_sem.at[slot_id], p).start()

    def hop(h):
        @pl.when(z >= h)
        def _():
            up(h - 1).wait_recv()

        if h < 3:
            @pl.when((z >= h) & (z < 3))
            def _():
                up(h).start()

        @pl.when(z + h <= 3)
        def _():
            down(h - 1).wait_recv()

        if h < 3:
            @pl.when((z + h <= 3) & (z > 0))
            def _():
                down(h).start()

        give(h)

    sends = []
    if relayed:
        @pl.when(z < 3)
        def _():
            up(0).start()

        @pl.when(z > 0)
        def _():
            down(0).start()

        give(0)
    else:
        for k in (7, 5, 6, 3, 4, 1, 2):
            c = remote(basis, shard.at[k], send_sem.at[k], recv_sem.at[k], (me + n - steps[k]) % n)
            c.start()
            sends.append(c)
    for c in small:
        c.wait()

    away = owner[...] - me
    away = jnp.where(away < 0, away + n, away)
    key = jnp.zeros_like(away)
    for k in range(1, 8):
        key = jnp.where(away == steps[k], k, key)
    place = key * 16 + offset[...] * 4 + rows[...]
    slot = lax.broadcasted_iota(jnp.int32, (1, CAP), 1)
    place = jnp.where(slot < count[0], place, -1)
    p_ids = lax.broadcasted_iota(jnp.int32, (CAP, CAP), 0)
    lane = lax.broadcasted_iota(jnp.int32, (CAP, CAP), 1)
    swapped = jnp.where((p_ids // 4) % 2 == 0, p_ids + 4, p_ids - 4)
    hot = jnp.concatenate([(p_ids == place), (swapped == place)], axis=0)
    hot = jnp.where(hot, 1.0, 0.0).astype(BF16)
    hot = jnp.concatenate([hot, hot], axis=1)
    keep = (p_ids // 4) % 2 == lane // B

    tang_copy.wait()

    def build(it, _):
        t = tang[:, pl.ds(pl.multiple_of(it * 256, 256), 256)]
        t_hi, t_lo = split(t)
        e = mm(hot, jnp.concatenate([t_hi, t_lo], axis=0))
        out = []
        for m in range(2):
            a = e[:CAP, m * 128:(m + 1) * 128]
            b = pltpu.roll(e[CAP:, m * 128:(m + 1) * 128], B, 1)
            out.append(jnp.where(keep, a, b))
        at_row = pl.ds(pl.multiple_of(it * 16, 16), 16)
        for cp in range(16):
            x = jnp.concatenate([out[0][cp * 8:cp * 8 + 8], out[1][cp * 8:cp * 8 + 8]], axis=0)
            hi, lo = split(x)
            dense_hi[at_row, cp * 128:(cp + 1) * 128] = hi
            dense_lo[at_row, cp * 128:(cp + 1) * 128] = lo
        return 0

    lax.fori_loop(0, 6, build, 0)
    if relayed:
        hop(1)
    lax.fori_loop(6, 16, build, 0)
    if relayed:
        hop(2)

    own_copy.wait()
    own = shard[own_slot]
    t_hi, t_lo = split(own.T)
    eye = p_ids == lane
    spring = jnp.concatenate(
        [jnp.sum(jnp.where(eye, springs[h:h + 1, :], 0.0), axis=1, keepdims=True) for h in range(2)], axis=0
    )
    scaled = spring * own

    def term(k, g):
        g_hi, g_lo = split(g)
        ks = slice(k * 256, (k + 1) * 256)
        return mm3(dense_hi[:, ks], dense_lo[:, ks], g_hi, g_lo)

    total = term(0, own)
    if relayed:
        hop(3)
        for k, ahead in ((3, 1), (4, 3), (7, 2)):
            total = total + term(k, shard[(z + ahead) % 4])
        order = ((1, 4), (2, 6), (5, 5), (6, 7))
    else:
        order = [(k, k) for k in range(1, 8)]
    for k, slot_id in order:
        remote(basis, shard.at[slot_id], send_sem.at[slot_id], recv_sem.at[slot_id], mate(1)).wait_recv()
        total = total + term(k, shard[slot_id])
    acc[...] = total
    image = scaled + jnp.concatenate([acc[pl.ds(r, B, stride=BR_DEV), :] for r in range(BR_DEV)], axis=0)
    stiff[...] = image
    i_hi, i_lo = split(image)
    part[...] = (mm3(t_hi, t_lo, i_hi, i_lo) * (1.0 / dof_total)).reshape(SUB, 8, MODES)

    rs = []
    for s in range(1, SUB):
        c = pltpu.make_async_remote_copy(
            part.at[(pos + s) % SUB], rs_buf.at[s], rs_send.at[s], rs_recv.at[s],
            device_id=at(mate(s)), device_id_type=pl.DeviceIdType.MESH,
        )
        c.start()
        rs.append(c)
    mine = part[pos]
    for s in range(1, SUB):
        rs[s - 1].wait_recv()
        mine = mine + rs_buf[s]
    if subs > 1:
        top_buf[sub] = mine
        top = []
        for q in range(1, subs):
            c = pltpu.make_async_remote_copy(
                top_buf.at[sub], top_buf.at[sub], top_send.at[q], top_recv.at[q],
                device_id=at((me + SUB * q) % n), device_id_type=pl.DeviceIdType.MESH,
            )
            c.start()
            top.append(c)
        for c in top:
            c.wait_recv()
        mine = top_buf[0]
        for q in range(1, subs):
            mine = mine + top_buf[q]
    red[pos] = mine
    ag = []
    for s in range(1, SUB):
        c = pltpu.make_async_remote_copy(
            red.at[pos], red.at[pos], ag_send.at[s], ag_recv.at[s],
            device_id=at(mate(s)), device_id_type=pl.DeviceIdType.MESH,
        )
        c.start()
        ag.append(c)
    for c in ag:
        c.wait_recv()
    reduced[...] = red[...].reshape(MODES, MODES)
    if relayed:
        for h in range(3):
            @pl.when((z >= h) & (z < 3))
            def _(h=h):
                up(h).wait_send()

            @pl.when((z + h <= 3) & (z > 0))
            def _(h=h):
                down(h).wait_send()

        for slot_id in range(4, 8):
            remote(
                basis, shard.at[slot_id], send_sem.at[slot_id], recv_sem.at[slot_id], mate(1)
            ).wait_send()
    for c in sends:
        c.wait_send()
    for c in rs + ag:
        c.wait_send()
    if subs > 1:
        for c in top:
            c.wait_send()


def shards(basis, springs, tangent_blocks, tile_rows, tile_owner, tile_offset, tile_count):
    n = lax.axis_size("row")
    dof_total = basis.shape[0] * n
    vm = pl.BlockSpec(memory_space=pltpu.VMEM)
    hbm = pl.BlockSpec(memory_space=pl.ANY)
    subs = max(n // SUB, 2)
    return pl.pallas_call(
        functools.partial(kernel, n, dof_total),
        out_shape=(
            jax.ShapeDtypeStruct((BR_DEV * B, MODES), F32),
            jax.ShapeDtypeStruct((MODES, MODES), F32),
        ),
        in_specs=[hbm] * 6 + [pl.BlockSpec(memory_space=pltpu.SMEM)],
        out_specs=(vm, vm),
        scratch_shapes=[
            pltpu.VMEM((2, MODES), F32),
            pltpu.VMEM((1, CAP), jnp.int32),
            pltpu.VMEM((1, CAP), jnp.int32),
            pltpu.VMEM((1, CAP), jnp.int32),
            pltpu.VMEM((8, BR_DEV * B, MODES), F32),
            pltpu.VMEM((CAP, B * B), F32),
            pltpu.VMEM((BR_DEV * B, 32 * B), BF16),
            pltpu.VMEM((BR_DEV * B, 32 * B), BF16),
            pltpu.VMEM((BR_DEV * B, MODES), F32),
            pltpu.VMEM((SUB, 8, MODES), F32),
            pltpu.VMEM((SUB, 8, MODES), F32),
            pltpu.VMEM((subs, 8, MODES), F32),
            pltpu.VMEM((SUB, 8, MODES), F32),
            pltpu.SemaphoreType.DMA((6,)),
            pltpu.SemaphoreType.DMA((8,)),
            pltpu.SemaphoreType.DMA((8,)),
            pltpu.SemaphoreType.DMA((3,)),
            pltpu.SemaphoreType.DMA((3,)),
            pltpu.SemaphoreType.DMA((3,)),
            pltpu.SemaphoreType.DMA((3,)),
            pltpu.SemaphoreType.DMA((SUB,)),
            pltpu.SemaphoreType.DMA((SUB,)),
            pltpu.SemaphoreType.DMA((subs,)),
            pltpu.SemaphoreType.DMA((subs,)),
            pltpu.SemaphoreType.DMA((SUB,)),
            pltpu.SemaphoreType.DMA((SUB,)),
        ],
        compiler_params=pltpu.CompilerParams(
            collective_id=0, has_side_effects=True, vmem_limit_bytes=60 * 1024 * 1024
        ),
    )(
        basis, springs.reshape(2, MODES), tangent_blocks,
        tile_rows.reshape(1, CAP), tile_owner.reshape(1, CAP), tile_offset.reshape(1, CAP), tile_count,
    )


def solution(mesh):
    in_specs = (
        P(("groups", "row"), None),
        P(("groups", "row")),
        P(("groups", "row"), None),
        P(("groups", "row")),
        P(("groups", "row"), None),
        P(("groups", "row")),
        P(("groups", "row")),
    )
    out_specs = (P(("groups", "row"), None), P("groups", None))
    return jax.shard_map(shards, mesh=mesh, in_specs=in_specs, out_specs=out_specs, check_vma=False)
```

```python
import functools

import jax
import jax.numpy as jnp
from jax import lax
from jax.experimental import pallas as pl
from jax.experimental.pallas import tpu as pltpu
from jax.sharding import PartitionSpec as P

B = 64
MODES = 128
BR_DEV = 4
CAP = 128
F32, BF16 = jnp.float32, jnp.bfloat16


def split(x):
    hi = x.astype(BF16)
    return hi, (x - hi.astype(F32)).astype(BF16)


def mm(a, b):
    return jnp.dot(a, b, preferred_element_type=F32)


def mm3(a_hi, a_lo, b_hi, b_lo):
    both = mm(a_hi, jnp.concatenate([b_hi, b_lo], axis=1))
    return both[:, :MODES] + both[:, MODES:] + mm(a_lo, b_hi)


def kernel(
    n, dof_total,
    basis, springs_in, tangent, rows_in, owner_in, offset_in, count,
    stiff, reduced,
    springs, rows, owner, offset,
    shard, tang, dense_hi, dense_lo, acc, part, rs_buf, top_buf, red,
    loc_sem, send_sem, recv_sem, up_send, up_recv, down_send, down_recv, rs_send, rs_recv, top_send, top_recv, ag_send, ag_recv,
):
    me = lax.axis_index("row")
    steps = (0, 1, n - 1, 4, n - 4, 5, n - 5, n // 2)
    planes = n // 4
    z, q = me // 4, me % 4
    relayed = n == 16

    def at(p):
        return {"row": p}

    def mate(s):
        return z * 4 + (q + s) % 4

    barrier = pltpu.get_barrier_semaphore()
    greeted = [mate(s) for s in range(1, 4)] + [(me + 4 * s) % n for s in range(1, planes)]
    if not relayed:
        greeted += [(me + o) % n for o in steps[1:]]
    for p in greeted:
        pl.semaphore_signal(barrier, inc=1, device_id=at(p), device_id_type=pl.DeviceIdType.MESH)
    own_slot = z if relayed else 0
    own_copy = pltpu.make_async_copy(basis, shard.at[own_slot], loc_sem.at[0])
    own_copy.start()
    small = [
        pltpu.make_async_copy(x, y, loc_sem.at[2 + i])
        for i, (x, y) in enumerate(((springs_in, springs), (rows_in, rows), (owner_in, owner), (offset_in, offset)))
    ]
    for c in small:
        c.start()
    tang_copy = pltpu.make_async_copy(tangent, tang, loc_sem.at[1])
    tang_copy.start()
    pl.semaphore_wait(barrier, len(greeted))

    def remote(src, dst, s_sem, r_sem, p):
        return pltpu.make_async_remote_copy(
            src, dst, s_sem, r_sem, device_id=at(p), device_id_type=pl.DeviceIdType.MESH
        )

    def half(ref, c):
        return ref.at[pl.ds(c * 128, 128)]

    def up(h, c):
        to = half(shard.at[(z - h) % 4], c)
        return remote(half(basis, c) if h == 0 else to, to, up_send.at[h, c], up_recv.at[h, c], (me + 4) % n)

    def down(h, c):
        to = half(shard.at[(z + h) % 4], c)
        return remote(half(basis, c) if h == 0 else to, to, down_send.at[h, c], down_recv.at[h, c], (me + n - 4) % n)

    def handed(src, slot_id, c, p):
        return remote(
            half(src, c), half(shard.at[slot_id], c), send_sem.at[slot_id, c], recv_sem.at[slot_id, c], p
        )

    first, last = jnp.where(q == 0, 1, 0), jnp.where(q == 3, 1, 0)
    gives = (
        (4, (z + first) % 4, z * 4 + (q + 3) % 4),
        (5, (z + 1 + first) % 4, z * 4 + (q + 3) % 4),
        (6, (z + 4 - last) % 4, z * 4 + (q + 1) % 4),
        (7, (z + 3 - last) % 4, z * 4 + (q + 1) % 4),
    )

    def give(h, c):
        for slot_id, whose, p in gives:
            far = jnp.where(whose < z, z - whose, whose - z)

            @pl.when(far == h)
            def _(slot_id=slot_id, whose=whose, p=p):
                handed(basis if h == 0 else shard.at[whose], slot_id, c, p).start()

    def hop(h):
        for c in range(2):
            @pl.when(z >= h)
            def _():
                up(h - 1, c).wait_recv()

            if h < 3:
                @pl.when((z >= h) & (z < 3))
                def _():
                    up(h, c).start()

            @pl.when(z + h <= 3)
            def _():
                down(h - 1, c).wait_recv()

            if h < 3:
                @pl.when((z + h <= 3) & (z > 0))
                def _():
                    down(h, c).start()

            give(h, c)

    sends = []
    if relayed:
        for c in range(2):
            @pl.when(z < 3)
            def _():
                up(0, c).start()

            @pl.when(z > 0)
            def _():
                down(0, c).start()

        for c in range(2):
            give(0, c)
    else:
        for k in range(1, 8):
            c = remote(basis, shard.at[k], send_sem.at[k, 0], recv_sem.at[k, 0], (me + n - steps[k]) % n)
            c.start()
            sends.append(c)
    for c in small:
        c.wait()

    away = owner[...] - me
    away = jnp.where(away < 0, away + n, away)
    key = jnp.zeros_like(away)
    for k in range(1, 8):
        key = jnp.where(away == steps[k], k, key)
    place = key * 16 + offset[...] * 4 + rows[...]
    slot = lax.broadcasted_iota(jnp.int32, (1, CAP), 1)
    place = jnp.where(slot < count[0], place, -1)
    p_ids = lax.broadcasted_iota(jnp.int32, (CAP, CAP), 0)
    lane = lax.broadcasted_iota(jnp.int32, (CAP, CAP), 1)
    swapped = jnp.where((p_ids // 4) % 2 == 0, p_ids + 4, p_ids - 4)
    hot = jnp.concatenate([(p_ids == place), (swapped == place)], axis=0)
    hot = jnp.where(hot, 1.0, 0.0).astype(BF16)
    hot = jnp.concatenate([hot, hot], axis=1)
    keep = (p_ids // 4) % 2 == lane // B

    tang_copy.wait()

    def build(it, _):
        t = tang[:, pl.ds(pl.multiple_of(it * 256, 256), 256)]
        t_hi, t_lo = split(t)
        e = mm(hot, jnp.concatenate([t_hi, t_lo], axis=0))
        out = []
        for m in range(2):
            a = e[:CAP, m * 128:(m + 1) * 128]
            b = pltpu.roll(e[CAP:, m * 128:(m + 1) * 128], B, 1)
            out.append(jnp.where(keep, a, b))
        at_row = pl.ds(pl.multiple_of(it * 16, 16), 16)
        for cp in range(16):
            x = jnp.concatenate([out[0][cp * 8:cp * 8 + 8], out[1][cp * 8:cp * 8 + 8]], axis=0)
            hi, lo = split(x)
            dense_hi[at_row, cp * 128:(cp + 1) * 128] = hi
            dense_lo[at_row, cp * 128:(cp + 1) * 128] = lo
        return 0

    lax.fori_loop(0, 6, build, 0)
    if relayed:
        hop(1)
    lax.fori_loop(6, 16, build, 0)
    if relayed:
        hop(2)

    own_copy.wait()
    own = shard[own_slot]
    t_hi, t_lo = split(own.T)
    eye = p_ids == lane
    spring = jnp.concatenate(
        [jnp.sum(jnp.where(eye, springs[h:h + 1, :], 0.0), axis=1, keepdims=True) for h in range(2)], axis=0
    )
    scaled = spring * own

    def term(k, g):
        g_hi, g_lo = split(g)
        ks = slice(k * 256, (k + 1) * 256)
        return mm3(dense_hi[:, ks], dense_lo[:, ks], g_hi, g_lo)

    total = term(0, own)
    if relayed:
        hop(3)
        for k, ahead in ((3, 1), (4, 3), (7, 2)):
            total = total + term(k, shard[(z + ahead) % 4])
        order = ((1, 4), (2, 6), (5, 5), (6, 7))
    else:
        order = [(k, k) for k in range(1, 8)]
    for k, slot_id in order:
        if relayed:
            for c in range(2):
                handed(basis, slot_id, c, mate(1)).wait_recv()
        else:
            sends[k - 1].wait_recv()
        total = total + term(k, shard[slot_id])
    acc[...] = total
    image = scaled + jnp.concatenate([acc[pl.ds(r, B, stride=BR_DEV), :] for r in range(BR_DEV)], axis=0)
    stiff[...] = image
    i_hi, i_lo = split(image)
    part[...] = (mm3(t_hi, t_lo, i_hi, i_lo) * (1.0 / dof_total)).reshape(4, MODES // 4, MODES)

    rs = [remote(part.at[(q + s) % 4], rs_buf.at[s], rs_send.at[s], rs_recv.at[s], mate(s)) for s in range(1, 4)]
    for c in rs:
        c.start()
    mine = part[q]
    for s in range(1, 4):
        rs[s - 1].wait_recv()
        mine = mine + rs_buf[s]
    top_buf[z] = mine
    top = [
        remote(top_buf.at[z], top_buf.at[z], top_send.at[s], top_recv.at[s], (me + 4 * s) % n)
        for s in range(1, planes)
    ]
    for c in top:
        c.start()
    for c in top:
        c.wait_recv()
    mine = top_buf[0]
    for s in range(1, planes):
        mine = mine + top_buf[s]
    red[q] = mine
    ag = [remote(red.at[q], red.at[q], ag_send.at[s], ag_recv.at[s], mate(s)) for s in range(1, 4)]
    for c in ag:
        c.start()
    for c in ag:
        c.wait_recv()
    reduced[...] = red[...].reshape(MODES, MODES)
    if relayed:
        for h, c in [(h, c) for h in range(3) for c in range(2)]:
            @pl.when((z >= h) & (z < 3))
            def _(h=h, c=c):
                up(h, c).wait_send()

            @pl.when((z + h <= 3) & (z > 0))
            def _(h=h, c=c):
                down(h, c).wait_send()

        for slot_id, c in [(i, c) for i in range(4, 8) for c in range(2)]:
            handed(basis, slot_id, c, mate(1)).wait_send()
    for c in sends:
        c.wait_send()
    for c in rs + top + ag:
        c.wait_send()


def shards(basis, springs, tangent_blocks, tile_rows, tile_owner, tile_offset, tile_count):
    n = lax.axis_size("row")
    dof_total = basis.shape[0] * n
    vm = pl.BlockSpec(memory_space=pltpu.VMEM)
    hbm = pl.BlockSpec(memory_space=pl.ANY)
    planes = n // 4
    return pl.pallas_call(
        functools.partial(kernel, n, dof_total),
        out_shape=(
            jax.ShapeDtypeStruct((BR_DEV * B, MODES), F32),
            jax.ShapeDtypeStruct((MODES, MODES), F32),
        ),
        in_specs=[hbm] * 6 + [pl.BlockSpec(memory_space=pltpu.SMEM)],
        out_specs=(vm, vm),
        scratch_shapes=[
            pltpu.VMEM((2, MODES), F32),
            pltpu.VMEM((1, CAP), jnp.int32),
            pltpu.VMEM((1, CAP), jnp.int32),
            pltpu.VMEM((1, CAP), jnp.int32),
            pltpu.VMEM((8, BR_DEV * B, MODES), F32),
            pltpu.VMEM((CAP, B * B), F32),
            pltpu.VMEM((BR_DEV * B, 32 * B), BF16),
            pltpu.VMEM((BR_DEV * B, 32 * B), BF16),
            pltpu.VMEM((BR_DEV * B, MODES), F32),
            pltpu.VMEM((4, MODES // 4, MODES), F32),
            pltpu.VMEM((4, MODES // 4, MODES), F32),
            pltpu.VMEM((planes, MODES // 4, MODES), F32),
            pltpu.VMEM((4, MODES // 4, MODES), F32),
            pltpu.SemaphoreType.DMA((6,)),
            pltpu.SemaphoreType.DMA((8, 2)),
            pltpu.SemaphoreType.DMA((8, 2)),
            pltpu.SemaphoreType.DMA((3, 2)),
            pltpu.SemaphoreType.DMA((3, 2)),
            pltpu.SemaphoreType.DMA((3, 2)),
            pltpu.SemaphoreType.DMA((3, 2)),
            pltpu.SemaphoreType.DMA((4,)),
            pltpu.SemaphoreType.DMA((4,)),
            pltpu.SemaphoreType.DMA((planes,)),
            pltpu.SemaphoreType.DMA((planes,)),
            pltpu.SemaphoreType.DMA((4,)),
            pltpu.SemaphoreType.DMA((4,)),
        ],
        compiler_params=pltpu.CompilerParams(
            collective_id=0, has_side_effects=True, vmem_limit_bytes=60 * 1024 * 1024
        ),
    )(
        basis, springs.reshape(2, MODES), tangent_blocks,
        tile_rows.reshape(1, CAP), tile_owner.reshape(1, CAP), tile_offset.reshape(1, CAP), tile_count,
    )


def solution(mesh):
    in_specs = (
        P(("groups", "row"), None),
        P(("groups", "row")),
        P(("groups", "row"), None),
        P(("groups", "row")),
        P(("groups", "row"), None),
        P(("groups", "row")),
        P(("groups", "row")),
    )
    out_specs = (P(("groups", "row"), None), P("groups", None))
    return jax.shard_map(shards, mesh=mesh, in_specs=in_specs, out_specs=out_specs, check_vma=False)
```

```python
import functools

import jax
import jax.numpy as jnp
from jax import lax
from jax.experimental import pallas as pl
from jax.experimental.pallas import tpu as pltpu
from jax.sharding import PartitionSpec as P

B = 64
MODES = 128
BR_DEV = 4
CAP = 128
PIECES = 4
PIECE = BR_DEV * B // PIECES
F32, BF16 = jnp.float32, jnp.bfloat16


def split(x):
    hi = x.astype(BF16)
    return hi, (x - hi.astype(F32)).astype(BF16)


def mm(a, b):
    return jnp.dot(a, b, preferred_element_type=F32)


def mm3(a_hi, a_lo, b_hi, b_lo):
    both = mm(a_hi, jnp.concatenate([b_hi, b_lo], axis=1))
    return both[:, :MODES] + both[:, MODES:] + mm(a_lo, b_hi)


def kernel(
    n, dof_total,
    basis, springs_in, tangent, rows_in, owner_in, offset_in, count_in,
    stiff, reduced,
    springs, rows, owner, offset, count,
    shard, tang, dense_hi, dense_lo, acc, acc2, part, rs_buf, top_buf, red,
    loc_sem, send_sem, recv_sem, up_send, up_recv, down_send, down_recv, rs_send, rs_recv, top_send, top_recv, ag_send, ag_recv,
):
    me = lax.axis_index("row")
    steps = (0, 1, n - 1, 4, n - 4, 5, n - 5, n // 2)
    planes = n // 4
    z, q = me // 4, me % 4
    relayed = n == 16

    def at(p):
        return {"row": p}

    def mate(s):
        return z * 4 + (q + s) % 4

    barrier = pltpu.get_barrier_semaphore()
    greeted = [mate(s) for s in range(1, 4)] + [(me + 4 * s) % n for s in range(1, planes)]
    if not relayed:
        greeted += [(me + o) % n for o in steps[1:]]
    for p in greeted:
        pl.semaphore_signal(barrier, inc=1, device_id=at(p), device_id_type=pl.DeviceIdType.MESH)
    own_slot = z if relayed else 0
    own_copy = pltpu.make_async_copy(basis, shard.at[own_slot], loc_sem.at[0])
    own_copy.start()
    small = [
        pltpu.make_async_copy(x, y, loc_sem.at[2 + i])
        for i, (x, y) in enumerate(((springs_in, springs), (rows_in, rows), (owner_in, owner), (offset_in, offset), (count_in, count)))
    ]
    for c in small:
        c.start()
    tang_copy = pltpu.make_async_copy(tangent, tang, loc_sem.at[1])
    tang_copy.start()
    pl.semaphore_wait(barrier, len(greeted))

    def remote(src, dst, s_sem, r_sem, p):
        return pltpu.make_async_remote_copy(
            src, dst, s_sem, r_sem, device_id=at(p), device_id_type=pl.DeviceIdType.MESH
        )

    def piece(ref, c):
        return ref.at[pl.ds(c * PIECE, PIECE)]

    def up(h, c):
        to = piece(shard.at[(z - h) % 4], c)
        return remote(piece(basis, c) if h == 0 else to, to, up_send.at[h, c], up_recv.at[h, c], (me + 4) % n)

    def down(h, c):
        to = piece(shard.at[(z + h) % 4], c)
        return remote(piece(basis, c) if h == 0 else to, to, down_send.at[h, c], down_recv.at[h, c], (me + n - 4) % n)

    def handed(src, slot_id, c, p):
        return remote(
            piece(src, c), piece(shard.at[slot_id], c), send_sem.at[slot_id, c], recv_sem.at[slot_id, c], p
        )

    first, last = jnp.where(q == 0, 1, 0), jnp.where(q == 3, 1, 0)
    gives = (
        (4, (z + first) % 4, z * 4 + (q + 3) % 4),
        (5, (z + 1 + first) % 4, z * 4 + (q + 3) % 4),
        (6, (z + 4 - last) % 4, z * 4 + (q + 1) % 4),
        (7, (z + 3 - last) % 4, z * 4 + (q + 1) % 4),
    )

    def give(h, c):
        for slot_id, whose, p in gives:
            far = jnp.where(whose < z, z - whose, whose - z)

            @pl.when(far == h)
            def _(slot_id=slot_id, whose=whose, p=p):
                handed(basis if h == 0 else shard.at[whose], slot_id, c, p).start()

    def hop(h):
        for c in range(PIECES):
            @pl.when(z >= h)
            def _():
                up(h - 1, c).wait_recv()

            if h < 3:
                @pl.when((z >= h) & (z < 3))
                def _():
                    up(h, c).start()

            @pl.when(z + h <= 3)
            def _():
                down(h - 1, c).wait_recv()

            if h < 3:
                @pl.when((z + h <= 3) & (z > 0))
                def _():
                    down(h, c).start()

            give(h, c)

    sends = []
    if relayed:
        for c in range(PIECES):
            @pl.when(z < 3)
            def _():
                up(0, c).start()

            @pl.when(z > 0)
            def _():
                down(0, c).start()

        for c in range(PIECES):
            give(0, c)
    else:
        for k in range(1, 8):
            c = remote(basis, shard.at[k], send_sem.at[k, 0], recv_sem.at[k, 0], (me + n - steps[k]) % n)
            c.start()
            sends.append(c)
    for c in small:
        c.wait()

    away = owner[...] - me
    away = jnp.where(away < 0, away + n, away)
    key = jnp.zeros_like(away)
    for k in range(1, 8):
        key = jnp.where(away == steps[k], k, key)
    place = key * 16 + offset[...] * 4 + rows[...]
    slot = lax.broadcasted_iota(jnp.int32, (1, CAP), 1)
    place = jnp.where(slot < count[0], place, -1)
    p_ids = lax.broadcasted_iota(jnp.int32, (CAP, CAP), 0)
    lane = lax.broadcasted_iota(jnp.int32, (CAP, CAP), 1)
    swapped = jnp.where((p_ids // 4) % 2 == 0, p_ids + 4, p_ids - 4)
    hot = jnp.concatenate([(p_ids == place), (swapped == place)], axis=0)
    hot = jnp.where(hot, 1.0, 0.0).astype(BF16)
    hot = jnp.concatenate([hot, hot], axis=1)
    keep = (p_ids // 4) % 2 == lane // B

    tang_copy.wait()

    def build(it, _):
        t = tang[:, pl.ds(pl.multiple_of(it * 256, 256), 256)]
        t_hi, t_lo = split(t)
        e = mm(hot, jnp.concatenate([t_hi, t_lo], axis=0))
        out = []
        for m in range(2):
            a = e[:CAP, m * 128:(m + 1) * 128]
            b = pltpu.roll(e[CAP:, m * 128:(m + 1) * 128], B, 1)
            out.append(jnp.where(keep, a, b))
        at_row = pl.ds(pl.multiple_of(it * 16, 16), 16)
        for cp in range(16):
            x = jnp.concatenate([out[0][cp * 8:cp * 8 + 8], out[1][cp * 8:cp * 8 + 8]], axis=0)
            hi, lo = split(x)
            dense_hi[at_row, cp * 128:(cp + 1) * 128] = hi
            dense_lo[at_row, cp * 128:(cp + 1) * 128] = lo
        return 0

    lax.fori_loop(0, 6, build, 0)
    if relayed:
        hop(1)
    lax.fori_loop(6, 16, build, 0)
    if relayed:
        hop(2)

    own_copy.wait()
    own = shard[own_slot]
    t_hi, t_lo = split(own.T)
    eye = p_ids == lane
    spring = jnp.concatenate(
        [jnp.sum(jnp.where(eye, springs[h:h + 1, :], 0.0), axis=1, keepdims=True) for h in range(2)], axis=0
    )
    scaled = spring * own

    def term(k, g):
        g_hi, g_lo = split(g)
        ks = slice(k * 256, (k + 1) * 256)
        return mm3(dense_hi[:, ks], dense_lo[:, ks], g_hi, g_lo)

    total = term(0, own)
    if relayed:
        hop(3)
        for k, ahead in ((3, 1), (4, 3), (7, 2)):
            total = total + term(k, shard[(z + ahead) % 4])
        order = ((1, 4), (2, 6), (5, 5), (6, 7))
    else:
        order = [(k, k) for k in range(1, 8)]
    for k, slot_id in order:
        if relayed:
            for c in range(PIECES):
                handed(basis, slot_id, c, mate(1)).wait_recv()
        else:
            sends[k - 1].wait_recv()
        total = total + term(k, shard[slot_id])
    acc[...] = total
    image = scaled + jnp.concatenate([acc[pl.ds(r, B, stride=BR_DEV), :] for r in range(BR_DEV)], axis=0)
    acc2[...] = image
    out_copy = pltpu.make_async_copy(acc2, stiff, loc_sem.at[0])
    out_copy.start()
    i_hi, i_lo = split(image)
    part[...] = (mm3(t_hi, t_lo, i_hi, i_lo) * (1.0 / dof_total)).reshape(4, MODES // 4, MODES)

    rs = [remote(part.at[(q + s) % 4], rs_buf.at[s], rs_send.at[s], rs_recv.at[s], mate(s)) for s in range(1, 4)]
    for c in rs:
        c.start()
    mine = part[q]
    for s in range(1, 4):
        rs[s - 1].wait_recv()
        mine = mine + rs_buf[s]
    top_buf[z] = mine
    top = [
        remote(top_buf.at[z], top_buf.at[z], top_send.at[s], top_recv.at[s], (me + 4 * s) % n)
        for s in range(1, planes)
    ]
    for c in top:
        c.start()
    for c in top:
        c.wait_recv()
    mine = top_buf[0]
    for s in range(1, planes):
        mine = mine + top_buf[s]
    red[q] = mine
    ag = [remote(red.at[q], red.at[q], ag_send.at[s], ag_recv.at[s], mate(s)) for s in range(1, 4)]
    for c in ag:
        c.start()
    for c in ag:
        c.wait_recv()
    reduced[...] = red[...].reshape(MODES, MODES)
    out_copy.wait()
    if relayed:
        for h, c in [(h, c) for h in range(3) for c in range(PIECES)]:
            @pl.when((z >= h) & (z < 3))
            def _(h=h, c=c):
                up(h, c).wait_send()

            @pl.when((z + h <= 3) & (z > 0))
            def _(h=h, c=c):
                down(h, c).wait_send()

        for slot_id, c in [(i, c) for i in range(4, 8) for c in range(PIECES)]:
            handed(basis, slot_id, c, mate(1)).wait_send()
    for c in sends:
        c.wait_send()
    for c in rs + top + ag:
        c.wait_send()


def shards(basis, springs, tangent_blocks, tile_rows, tile_owner, tile_offset, tile_count):
    n = lax.axis_size("row")
    dof_total = basis.shape[0] * n
    vm = pl.BlockSpec(memory_space=pltpu.VMEM)
    hbm = pl.BlockSpec(memory_space=pl.ANY)
    planes = n // 4
    return pl.pallas_call(
        functools.partial(kernel, n, dof_total),
        out_shape=(
            jax.ShapeDtypeStruct((BR_DEV * B, MODES), F32),
            jax.ShapeDtypeStruct((MODES, MODES), F32),
        ),
        in_specs=[hbm] * 7,
        out_specs=(hbm, vm),
        scratch_shapes=[
            pltpu.VMEM((2, MODES), F32),
            pltpu.VMEM((1, CAP), jnp.int32),
            pltpu.VMEM((1, CAP), jnp.int32),
            pltpu.VMEM((1, CAP), jnp.int32),
            pltpu.SMEM((1,), jnp.int32),
            pltpu.VMEM((8, BR_DEV * B, MODES), F32),
            pltpu.VMEM((CAP, B * B), F32),
            pltpu.VMEM((BR_DEV * B, 32 * B), BF16),
            pltpu.VMEM((BR_DEV * B, 32 * B), BF16),
            pltpu.VMEM((BR_DEV * B, MODES), F32),
            pltpu.VMEM((BR_DEV * B, MODES), F32),
            pltpu.VMEM((4, MODES // 4, MODES), F32),
            pltpu.VMEM((4, MODES // 4, MODES), F32),
            pltpu.VMEM((planes, MODES // 4, MODES), F32),
            pltpu.VMEM((4, MODES // 4, MODES), F32),
            pltpu.SemaphoreType.DMA((7,)),
            pltpu.SemaphoreType.DMA((8, PIECES)),
            pltpu.SemaphoreType.DMA((8, PIECES)),
            pltpu.SemaphoreType.DMA((3, PIECES)),
            pltpu.SemaphoreType.DMA((3, PIECES)),
            pltpu.SemaphoreType.DMA((3, PIECES)),
            pltpu.SemaphoreType.DMA((3, PIECES)),
            pltpu.SemaphoreType.DMA((4,)),
            pltpu.SemaphoreType.DMA((4,)),
            pltpu.SemaphoreType.DMA((planes,)),
            pltpu.SemaphoreType.DMA((planes,)),
            pltpu.SemaphoreType.DMA((4,)),
            pltpu.SemaphoreType.DMA((4,)),
        ],
        compiler_params=pltpu.CompilerParams(
            collective_id=0, has_side_effects=True, vmem_limit_bytes=60 * 1024 * 1024
        ),
    )(
        basis, springs.reshape(2, MODES), tangent_blocks,
        tile_rows.reshape(1, CAP), tile_owner.reshape(1, CAP), tile_offset.reshape(1, CAP), tile_count,
    )


def solution(mesh):
    in_specs = (
        P(("groups", "row"), None),
        P(("groups", "row")),
        P(("groups", "row"), None),
        P(("groups", "row")),
        P(("groups", "row"), None),
        P(("groups", "row")),
        P(("groups", "row")),
    )
    out_specs = (P(("groups", "row"), None), P("groups", None))
    return jax.shard_map(shards, mesh=mesh, in_specs=in_specs, out_specs=out_specs, check_vma=False)
```
